32 devices in a mesh: row: 8 (over y, x, core), col: 4 (over z).
Axes of the slice: x: 2, y: 2, z: 4, core: 2. Of those that a mesh axis runs over, the one named last changes fastest.
Arguments:
- core_inverse: bfloat16 [20480, 20480], P('row', 'col'), as said below
- core_noncore: bfloat16 [20480, 1024], P('row', 'col'), may hold values from -3 to 3
- residual: float32 [1024], replicated, may hold values from 8 to 64
- group_live: int32 [2], replicated, may hold values from 192 to 512, as said below
Outputs:
- core_block: float32 [20480, 20480], P('row', 'col')
The draws below stay inside these ranges and needn't reach their ends.
Inputs may be any that keep to these rules, and one draw needn't show every extreme that they name: core_inverse is exactly symmetric. `group_live`: in every draw one of the two groups holds 512 animals, the other at least 192.
All inputs are finite; a program needn't handle non-finite values.
Results may differ from the reference program's by a relative error of at most 0.0049.
Values may be sent and summed in bfloat16 or wider, within the bound.
No kernel may reach another device: no remote copies, remote signals or barrier semaphores. Data moves between devices by JAX's collectives and lax.ppermute only.
A program may use at most 192 MiB of HBM per device.

```python
import math
import jax
import jax.numpy as jnp
from jax import lax

NC = 20480
GROUP = 512
NN = 1024


def draw_core_inverse(key, part):
    first = jax.random.fold_in(jax.random.fold_in(key, 11), 0)
    noise = jax.random.normal(first, (NC, NC), jnp.float32)
    matrix = (noise + noise.T) / math.sqrt(2.0 * NC)
    scales = jnp.ones((NC,), jnp.float32)
    index = jnp.arange(NC)
    matrix = matrix.at[index, index].add(2.0 * scales)
    return matrix.astype(jnp.bfloat16)


def draw_group_live(key, part):
    first, second = jax.random.split(jax.random.fold_in(key, 5))
    full = jax.random.randint(first, (), 0, 2)
    other = jax.random.randint(second, (), GROUP * 3 // 8, GROUP + 1)
    return jnp.where(jnp.arange(2) == full, GROUP, other).astype(jnp.int32)


def block_scale(key, dims, shards, least, high):
    factor_of, own = 1.0, jax.random.fold_in(key, 6)
    for dim, parts in shards:
        draws = jnp.exp(jax.random.uniform(jax.random.fold_in(own, dim), (parts,), jnp.float32, least / len(shards), high / len(shards)))
        factor_of = factor_of * jnp.repeat(draws, dims[dim] // parts).reshape([-1 if axis == dim else 1 for axis in range(len(dims))])
    return factor_of


def bell_draw(own_key, extent, width, most, pieces=(), held_as=jnp.bfloat16):
    array = jax.random.normal(own_key, extent, jnp.float32) * width
    if len(pieces) > 0:
        array = block_scale(own_key, extent, pieces, -0.22, 0.18) * array
    return jnp.clip(array, min=-most, max=most).astype(held_as)


def setup_inputs(seed: int = 0) -> dict:
    key_list = jax.random.split(jax.random.key(seed), 5)
    return {
        "core_inverse": draw_core_inverse(jax.random.fold_in(key_list[4], 71), 0),
        "core_noncore": bell_draw(key_list[1], (NC, NN), 0.5, 3.0, ((0, 8), (1, 4))),
        "residual": jnp.clip(jnp.exp(jax.random.uniform(key_list[2], (NN,), jnp.float32, math.log(8.0), math.log(64.0))), 8.0, 64.0),
        "group_live": draw_group_live(jax.random.fold_in(key_list[4], 71), 0),
    }


def reference(core_inverse, core_noncore, residual, group_live):
    proj = jnp.dot(core_inverse, core_noncore, preferred_element_type=jnp.float32).astype(jnp.bfloat16)
    slots = jnp.arange(NN, dtype=jnp.int32)
    limit = jnp.where(slots // GROUP == 0, group_live[0], group_live[1])
    live = (slots % GROUP < limit).astype(jnp.float32)
    weight = live / residual
    scaled = (proj.astype(jnp.float32) * weight[None, :]).astype(jnp.bfloat16)
    update = lax.dot_general(scaled, proj, (((1,), (1,)), ((), ())), preferred_element_type=jnp.float32)
    return core_inverse.astype(jnp.float32) + update
```

```python
import functools

import jax
import jax.numpy as jnp
from jax import lax
from jax.experimental import pallas as pl
from jax.experimental.pallas import tpu as pltpu
from jax.sharding import PartitionSpec as P

GROUP = 512
BF16 = jnp.bfloat16
F32 = jnp.float32


VMEM = 60 * 2**20
PIECES = 1


def after(value, *others):
    return lax.optimization_barrier((value, *others))[0]


def largest_block(size, most):
    return max([b for b in range(16, most + 1, 16) if size % b == 0], default=size)


def send_kernel(ids, turned, core, out):
    out[...] = jnp.dot(turned[...], core[...], preferred_element_type=F32).astype(BF16)


def own_kernel(count, ids, turned, core, *refs):
    others, own, outs = refs[: -count - 1], refs[-count - 1], refs[-count:]
    i = pl.program_id(0)
    value = jnp.dot(turned[...], core[...], preferred_element_type=F32)
    for other in others:
        value = value + other[...].astype(F32)

    @pl.when(i == ids[0])
    def _():
        own[...] = value
        for out in outs:
            out[...] = jnp.zeros_like(out)

    @pl.when(i != ids[0])
    def _():
        depth = outs[0].shape[0]
        for n, out in enumerate(outs):
            out[...] = value[n * depth : (n + 1) * depth].astype(BF16)


def stage(kernel, ids, turned, core, mask, others, col_size, twins, out_specs, out_shape):
    slots, rows = turned.shape
    part = core.shape[1] // twins // col_size
    return pl.pallas_call(
        kernel,
        grid_spec=pltpu.PrefetchScalarGridSpec(
            num_scalar_prefetch=1,
            grid=(col_size,),
            in_specs=[
                pl.BlockSpec((slots, rows), lambda j, ids: (0, 0)),
                pl.BlockSpec(
                    (rows, part), lambda j, ids: (0, (ids[1] ^ mask) * col_size + j)
                ),
            ]
            + [pl.BlockSpec((slots, part), lambda j, ids: (0, j))] * len(others),
            out_specs=out_specs,
        ),
        out_shape=out_shape,
        cost_estimate=pl.CostEstimate(
            flops=2 * rows * slots * part * col_size,
            bytes_accessed=2 * rows * (part * col_size + slots),
            transcendentals=0,
        ),
        compiler_params=pltpu.CompilerParams(vmem_limit_bytes=VMEM),
        name="own" if others else "send",
    )(ids, turned, core, *others)


def send(ids, turned, core, col_size, twins, flip):
    slots = turned.shape[0]
    part = core.shape[1] // twins // col_size
    result = []
    for mask in range(1, twins):
        if part % 128:
            value = jnp.dot(turned, core, preferred_element_type=F32)
            value = value.reshape(slots, twins, col_size * part)
            value = lax.dynamic_index_in_dim(value, ids[1] ^ mask, 1, keepdims=False)
            value = value.astype(BF16)
        else:
            value = stage(
                send_kernel,
                ids,
                turned,
                core,
                mask,
                [],
                col_size,
                twins,
                pl.BlockSpec((slots, part), lambda j, ids: (0, j)),
                jax.ShapeDtypeStruct((slots, part * col_size), BF16),
            )
        result.append((value, flip(value, mask)))
    return result


def project(ids, turned, core, others, col_size, twins):
    others = [x[1] if isinstance(x, tuple) else x for x in others]
    slots = turned.shape[0]
    part = core.shape[1] // twins // col_size
    k, t = ids[0], ids[1]
    if part % 128:
        value = jnp.dot(turned, core, preferred_element_type=F32)
        value = value.reshape(slots, twins, col_size * part)
        total = lax.dynamic_index_in_dim(value, t, 1, keepdims=False)
        for other in others:
            total = total + other.astype(F32)
        total = jnp.moveaxis(total.reshape(slots, col_size, part), 1, 0)
        own = lax.dynamic_index_in_dim(total, k, 0, keepdims=False)
        mine = jnp.arange(col_size)[:, None, None] == k
        total = jnp.where(mine, 0, total).astype(BF16)
        return own, jnp.split(total, PIECES, axis=1)
    own, *outs = stage(
        functools.partial(own_kernel, PIECES),
        ids,
        turned,
        core,
        0,
        others,
        col_size,
        twins,
        [
            pl.BlockSpec((slots, part), lambda j, ids: (0, 0)),
        ]
        + [pl.BlockSpec((None, slots // PIECES, part), lambda j, ids: (j, 0, 0))] * PIECES,
        [
            jax.ShapeDtypeStruct((slots, part), F32),
        ]
        + [jax.ShapeDtypeStruct((col_size, slots // PIECES, part), BF16)] * PIECES,
    )
    return own, outs


def finish_kernel(own, *refs):
    others, out = refs[:-1], refs[-1]
    depth = others[0].shape[1]
    for n, other in enumerate(others):
        rows = slice(n * depth, (n + 1) * depth)
        value = own[rows, :]
        for i in range(other.shape[0]):
            value = value + other[i].astype(F32)
        out[rows, :] = value.astype(BF16)


def finish(own, others):
    size = sum(x.size for x in others)
    return pl.pallas_call(
        finish_kernel,
        out_shape=jax.ShapeDtypeStruct(own.shape, BF16),
        cost_estimate=pl.CostEstimate(
            flops=size, bytes_accessed=6 * own.size + 2 * size, transcendentals=0
        ),
        compiler_params=pltpu.CompilerParams(vmem_limit_bytes=VMEM),
        name="finish",
    )(own, *others)


def update_kernel(twins, spans, ids, live, *refs):
    masks = len(refs) - 7
    pieces, (residual, base, source, out) = refs[:masks], refs[masks:-3]
    scaled, panel, sems = refs[-3:]
    depth, part = pieces[0].shape
    block = out.shape[0]

    @pl.when(pl.program_id(0) == 0)
    def _():
        count, _, cols = source.shape
        copies = []
        for r in range(count):
            place = r % twins * (count // twins) + r // twins if count > 1 else 0
            copies.append(
                pltpu.make_async_copy(
                    source.at[r], panel.at[:, pl.ds(place * cols, cols)], sems.at[r]
                )
            )
        for copy in copies:
            copy.start()
        slot = lax.broadcasted_iota(jnp.int32, residual.shape, 1)
        limit = jnp.where(slot < GROUP, live[0], live[1])
        inside = jnp.where(slot < GROUP, slot, slot - GROUP)
        weight = (inside < limit).astype(F32) / residual[...]
        weight = jnp.concatenate([weight[:, a:b] for a, b in spans], axis=1)
        for p, piece in enumerate(pieces):
            value = piece[...].T.astype(F32) * weight
            scaled[p * part : (p + 1) * part, :] = value.astype(BF16)
        for copy in copies:
            copy.wait()

    rows = pl.ds(pl.multiple_of(pl.program_id(0) * block, block), block)
    out[...] = base[...].astype(F32) + jnp.dot(
        scaled[rows, :], panel[...], preferred_element_type=F32
    )


def update(base, pieces, masks, spans, residual, panel, ids, live, twins):
    first, step = masks[0], masks[1] - masks[0]
    depth, part = pieces[0].shape
    rows, cols = base.shape
    block = largest_block(part, 128)
    steps = part // block

    def index(i, ids, live):
        place = ids[0] ^ ids[2] ^ (first + step * (i // steps))
        return place * steps + i % steps, 0

    tile = pl.BlockSpec((block, cols), index)
    operands = [*pieces, residual]
    in_specs = [pl.BlockSpec(x.shape, lambda i, *_: (0, 0)) for x in operands]
    return pl.pallas_call(
        functools.partial(update_kernel, twins, spans),
        grid_spec=pltpu.PrefetchScalarGridSpec(
            num_scalar_prefetch=2,
            grid=(len(masks) * steps,),
            in_specs=[*in_specs, tile, pl.BlockSpec(memory_space=pl.ANY)],
            out_specs=tile,
            scratch_shapes=[
                pltpu.VMEM((len(masks) * part, depth), BF16),
                pltpu.VMEM((depth, cols), BF16),
                pltpu.SemaphoreType.DMA((panel.shape[0],)),
            ],
        ),
        out_shape=jax.ShapeDtypeStruct((rows, cols), F32),
        input_output_aliases={2 + len(operands): 0} if base.dtype == F32 else {},
        cost_estimate=pl.CostEstimate(
            flops=2 * len(masks) * part * cols * depth,
            bytes_accessed=len(masks) * part * cols * 6 + 2 * cols * depth,
            transcendentals=0,
        ),
        compiler_params=pltpu.CompilerParams(vmem_limit_bytes=VMEM),
        name="update",
    )(ids, live, *operands, base, panel)


def shards(row_size, col_size, core_inverse, core_noncore, residual, group_live):
    rows, cols = core_inverse.shape
    width = core_noncore.shape[1]
    twins = row_size // col_size
    part = rows // col_size
    row, z = lax.axis_index("row"), lax.axis_index("col")
    k, t = row // twins, row % twins
    ids = jnp.stack([k, t, z]).astype(jnp.int32)

    def flip(value, mask):
        return lax.ppermute(value, "row", [(r, r ^ mask) for r in range(row_size)])

    def cross(value, mask):
        pairs = []
        for r in range(row_size):
            for c in range(col_size):
                to_row = c * twins + r % twins
                to_col = (r // twins) ^ c ^ mask
                pairs.append((r * col_size + c, to_row * col_size + to_col))
        return lax.ppermute(value, ("row", "col"), pairs)

    def exchange(value):
        plane = [
            [c * twins + twin for c in range(col_size)] for twin in range(twins)
        ]
        return lax.all_to_all(value, "row", 0, 0, axis_index_groups=plane)

    half = width // 2
    batches = [list(range(0, col_size, 2)), list(range(1, col_size, 2))]
    turned = core_noncore.T
    animals = [
        lax.all_gather(turned[i * half : (i + 1) * half], "col", axis=0, tiled=True)
        for i in range(2)
    ]

    sent = send(ids, animals[0], core_inverse, col_size, twins, flip)
    own, others = project(ids, animals[0], core_inverse, sent, col_size, twins)
    others = [exchange(x) for x in others]
    sent = send(ids, animals[1], core_inverse, col_size, twins, flip)
    groups = [finish(after(own, *[x[0] for x in sent]), others)]
    first = after(groups[0], animals[1])
    crossed = [[cross(first, mask)] for mask in range(col_size)]
    own, others = project(
        ids, animals[1], core_inverse, [x[1] for x in sent], col_size, twins
    )
    others = [exchange(x) for x in others]
    groups.append(finish(after(own, *[x[0] for x in crossed]), others))
    for mask in range(col_size):
        crossed[mask].append(cross(groups[1], mask))
    panels = []
    for group in groups:
        panel = lax.all_gather(group, "row", axis=0)
        if part % 128:
            panel = panel.reshape(col_size, twins, *group.shape)
            panel = jnp.transpose(panel, (2, 1, 0, 3)).reshape(1, -1, cols)
        panels.append(panel)

    out = core_inverse
    for number, batch in ((0, list(range(col_size))), (1, batches[0]), (1, batches[1])):
        starts = [q * width + number * half for q in range(col_size)]
        out = update(
            out,
            [crossed[mask][number] for mask in batch],
            batch,
            [(a, a + half) for a in starts],
            residual[None, :],
            panels[number],
            ids,
            group_live,
            twins,
        )
    return out


def solution(mesh):
    return jax.shard_map(
        functools.partial(shards, mesh.shape["row"], mesh.shape["col"]),
        mesh=mesh,
        in_specs=(P("row", "col"), P("row", "col"), P(), P()),
        out_specs=P("row", "col"),
        check_vma=False,
    )
```

```python
import functools

import jax
import jax.numpy as jnp
from jax import lax
from jax.experimental import pallas as pl
from jax.experimental.pallas import tpu as pltpu
from jax.sharding import PartitionSpec as P

GROUP = 512
BF16 = jnp.bfloat16
F32 = jnp.float32


VMEM = 127 * 2**19


def after(value, *others):
    return lax.optimization_barrier((value, *others))[0]


def largest_block(size, most):
    return max([b for b in range(16, most + 1, 16) if size % b == 0], default=size)


def send_kernel(ids, turned, core, out):
    out[...] = jnp.dot(turned[...], core[...], preferred_element_type=F32).astype(BF16)


def own_kernel(ids, turned, core, *refs):
    others, (own, out) = refs[:-2], refs[-2:]
    i = pl.program_id(0)
    value = jnp.dot(turned[...], core[...], preferred_element_type=F32)
    for other in others:
        value = value + other[...].astype(F32)

    @pl.when(i == ids[0])
    def _():
        own[...] = value
        out[...] = jnp.zeros_like(out)

    @pl.when(i != ids[0])
    def _():
        out[...] = value.astype(BF16)


def stage(kernel, ids, turned, core, mask, others, col_size, twins, out_specs, out_shape):
    slots, rows = turned.shape
    part = core.shape[1] // twins // col_size
    return pl.pallas_call(
        kernel,
        grid_spec=pltpu.PrefetchScalarGridSpec(
            num_scalar_prefetch=1,
            grid=(col_size,),
            in_specs=[
                pl.BlockSpec((slots, rows), lambda j, ids: (0, 0)),
                pl.BlockSpec(
                    (rows, part), lambda j, ids: (0, (ids[1] ^ mask) * col_size + j)
                ),
            ]
            + [pl.BlockSpec((slots, part), lambda j, ids: (0, j))] * len(others),
            out_specs=out_specs,
        ),
        out_shape=out_shape,
        cost_estimate=pl.CostEstimate(
            flops=2 * rows * slots * part * col_size,
            bytes_accessed=2 * rows * (part * col_size + slots),
            transcendentals=0,
        ),
        compiler_params=pltpu.CompilerParams(vmem_limit_bytes=VMEM),
        name="own" if others else "send",
    )(ids, turned, core, *others)


def send(ids, turned, core, col_size, twins, flip):
    slots = turned.shape[0]
    part = core.shape[1] // twins // col_size
    result = []
    for mask in range(1, twins):
        if part % 128:
            value = jnp.dot(turned, core, preferred_element_type=F32)
            value = value.reshape(slots, twins, col_size * part)
            value = lax.dynamic_index_in_dim(value, ids[1] ^ mask, 1, keepdims=False)
            value = value.astype(BF16)
        else:
            value = stage(
                send_kernel,
                ids,
                turned,
                core,
                mask,
                [],
                col_size,
                twins,
                pl.BlockSpec((slots, part), lambda j, ids: (0, j)),
                jax.ShapeDtypeStruct((slots, part * col_size), BF16),
            )
        result.append((value, flip(value, mask)))
    return result


def project(ids, turned, core, others, col_size, twins):
    others = [x[1] if isinstance(x, tuple) else x for x in others]
    slots = turned.shape[0]
    part = core.shape[1] // twins // col_size
    k, t = ids[0], ids[1]
    if part % 128:
        value = jnp.dot(turned, core, preferred_element_type=F32)
        value = value.reshape(slots, twins, col_size * part)
        total = lax.dynamic_index_in_dim(value, t, 1, keepdims=False)
        for other in others:
            total = total + other.astype(F32)
        total = jnp.moveaxis(total.reshape(slots, col_size, part), 1, 0)
        own = lax.dynamic_index_in_dim(total, k, 0, keepdims=False)
        mine = jnp.arange(col_size)[:, None, None] == k
        return own, jnp.where(mine, 0, total).astype(BF16)
    return stage(
        own_kernel,
        ids,
        turned,
        core,
        0,
        others,
        col_size,
        twins,
        [
            pl.BlockSpec((slots, part), lambda j, ids: (0, 0)),
            pl.BlockSpec((None, slots, part), lambda j, ids: (j, 0, 0)),
        ],
        [
            jax.ShapeDtypeStruct((slots, part), F32),
            jax.ShapeDtypeStruct((col_size, slots, part), BF16),
        ],
    )


def finish_kernel(own, others, out):
    value = own[...]
    for i in range(others.shape[0]):
        value = value + others[i].astype(F32)
    out[...] = value.astype(BF16)


def finish(own, others):
    return pl.pallas_call(
        finish_kernel,
        out_shape=jax.ShapeDtypeStruct(own.shape, BF16),
        cost_estimate=pl.CostEstimate(
            flops=others.size,
            bytes_accessed=6 * own.size + 2 * others.size,
            transcendentals=0,
        ),
        compiler_params=pltpu.CompilerParams(vmem_limit_bytes=VMEM),
        name="finish",
    )(own, others)


def update_kernel(masks, twins, spans, places, ids, live, *refs):
    halves = refs[:masks], refs[masks : 2 * masks]
    residual, core, *sources = refs[2 * masks : -4]
    out, scaled, panel, sems = refs[-4:]
    depth, part = halves[0][0].shape
    block = out.shape[0]

    @pl.when(pl.program_id(0) == 0)
    def _():
        copies = []
        for n, (first, twin) in enumerate(places):
            source = sources[n]
            count, height, cols = source.shape
            for r in range(count):
                if twin is None:
                    place = r % twins * (count // twins) + r // twins if count > 1 else 0
                    lane = place * cols
                else:
                    place = (ids[1] ^ twin) * count + (ids[0] ^ r)
                    lane = pl.multiple_of(place * cols, cols)
                copies.append(
                    pltpu.make_async_copy(
                        source.at[r],
                        panel.at[pl.ds(first, height), pl.ds(lane, cols)],
                        sems.at[len(copies)],
                    )
                )
        for copy in copies:
            copy.start()
        slot = lax.broadcasted_iota(jnp.int32, residual.shape, 1)
        limit = jnp.where(slot < GROUP, live[0], live[1])
        inside = jnp.where(slot < GROUP, slot, slot - GROUP)
        weight = (inside < limit).astype(F32) / residual[...]
        weight = jnp.concatenate([weight[:, a:b] for a, b in spans], axis=1)
        for g, pieces in enumerate(halves):
            lanes = slice(g * depth, (g + 1) * depth)
            for p, piece in enumerate(pieces):
                value = piece[...].T.astype(F32) * weight[:, lanes]
                scaled[p * part : (p + 1) * part, lanes] = value.astype(BF16)
        for copy in copies:
            copy.wait()

    rows = pl.ds(pl.multiple_of(pl.program_id(0) * block, block), block)
    out[...] = core[...].astype(F32) + jnp.dot(
        scaled[rows, :], panel[...], preferred_element_type=F32
    )


def update(core, stacked, pieces, spans, residual, panels, places, ids, live, twins):
    masks = len(pieces)
    depth, part = pieces[0].shape
    rows, cols = core.shape
    slots = residual.shape[1]
    block = largest_block(part, 320)
    steps = part // block

    def stacked_index(mask):
        return lambda i, ids, live: (ids[0] ^ ids[2] ^ mask, 0, 0)

    tile = pl.BlockSpec(
        (block, cols),
        lambda i, ids, live: ((ids[0] ^ ids[2] ^ (i // steps)) * steps + i % steps, 0),
    )
    once = pl.Buffered(1)
    in_specs = [
        pl.BlockSpec((None, depth, part), stacked_index(mask), pipeline_mode=once)
        for mask in range(masks)
    ]
    in_specs += [
        pl.BlockSpec(x.shape, lambda i, *_: (0, 0), pipeline_mode=once) for x in pieces
    ]
    in_specs += [pl.BlockSpec(residual.shape, lambda i, *_: (0, 0)), tile]
    in_specs += [pl.BlockSpec(memory_space=pl.ANY)] * len(panels)
    return pl.pallas_call(
        functools.partial(update_kernel, masks, twins, spans, places),
        grid_spec=pltpu.PrefetchScalarGridSpec(
            num_scalar_prefetch=2,
            grid=(masks * steps,),
            in_specs=in_specs,
            out_specs=tile,
            scratch_shapes=[
                pltpu.VMEM((masks * part, slots), BF16),
                pltpu.VMEM((slots, cols), BF16),
                pltpu.SemaphoreType.DMA((sum(x.shape[0] for x in panels),)),
            ],
        ),
        out_shape=jax.ShapeDtypeStruct((rows, cols), F32),
        cost_estimate=pl.CostEstimate(
            flops=2 * rows * cols * slots,
            bytes_accessed=rows * cols * 6 + 2 * cols * slots,
            transcendentals=0,
        ),
        compiler_params=pltpu.CompilerParams(vmem_limit_bytes=VMEM),
        name="update",
    )(ids, live, *[stacked] * masks, *pieces, residual, core, *panels)


def shards(row_size, col_size, core_inverse, core_noncore, residual, group_live):
    rows, cols = core_inverse.shape
    width = core_noncore.shape[1]
    twins = row_size // col_size
    part = rows // col_size
    row, z = lax.axis_index("row"), lax.axis_index("col")
    k, t = row // twins, row % twins
    ids = jnp.stack([k, t, z]).astype(jnp.int32)

    def flip(value, mask):
        return lax.ppermute(value, "row", [(r, r ^ mask) for r in range(row_size)])

    def cross(value, mask):
        pairs = []
        for r in range(row_size):
            for c in range(col_size):
                to_row = c * twins + r % twins
                to_col = (r // twins) ^ c ^ mask
                pairs.append((r * col_size + c, to_row * col_size + to_col))
        return lax.ppermute(value, ("row", "col"), pairs)

    def exchange(value):
        plane = [
            [c * twins + twin for c in range(col_size)] for twin in range(twins)
        ]
        return lax.all_to_all(value, "row", 0, 0, axis_index_groups=plane)

    half = width // 2
    turned = core_noncore.T
    animals = [
        lax.all_gather(turned[i * half : (i + 1) * half], "col", axis=0, tiled=True)
        for i in range(2)
    ]

    def gather_plane(group):
        panel = lax.all_gather(group, "row", axis=0)
        if part % 128:
            panel = panel.reshape(col_size, twins, *group.shape)
            panel = jnp.transpose(panel, (2, 1, 0, 3)).reshape(1, -1, cols)
        return panel

    sent = send(ids, animals[0], core_inverse, col_size, twins, flip)
    own, others = project(ids, animals[0], core_inverse, sent, col_size, twins)
    others = exchange(others)
    sent = send(ids, animals[1], core_inverse, col_size, twins, flip)
    first = finish(after(own, *[x[0] for x in sent]), others)
    levels = lax.all_gather(first, "col", axis=0)
    own, others = project(ids, animals[1], core_inverse, sent, col_size, twins)
    flipped, panels = [], []
    if part % 128 == 0:
        masks = [1 << bit for bit in range(col_size.bit_length() - 1)]
        near = {mask: flip(first, mask * twins) for mask in masks}
        others = after(others, *near.values())
        for mask in range(1, col_size):
            if mask in near:
                flipped.append(near[mask])
            elif mask.bit_count() == 2:
                one = mask & -mask
                cut = first.shape[0] // 2
                flipped.append(
                    jnp.concatenate(
                        [
                            flip(near[one][:cut], (mask ^ one) * twins),
                            flip(near[mask ^ one][cut:], one * twins),
                        ]
                    )
                )
            else:
                flipped.append(flip(first, mask * twins))
        held = jnp.stack([first, *flipped])
        panels = [held] + [flip(held, twin) for twin in range(1, twins)]
    second = finish(own, exchange(others))
    crossed = [cross(second, mask) for mask in range(col_size)]
    stacked = exchange(levels)
    if flipped:
        places = [(0, twin) for twin in range(twins)]
        panels.append(gather_plane(second))
        places.append((first.shape[0], None))
    else:
        panels = [gather_plane(jnp.concatenate([first, second], axis=0))]
        places = [(0, None)]

    starts = [q * width + g * half for g in range(2) for q in range(col_size)]
    return update(
        core_inverse,
        stacked,
        crossed,
        [(a, a + half) for a in starts],
        residual[None, :],
        panels,
        places,
        ids,
        group_live,
        twins,
    )


def solution(mesh):
    return jax.shard_map(
        functools.partial(shards, mesh.shape["row"], mesh.shape["col"]),
        mesh=mesh,
        in_specs=(P("row", "col"), P("row", "col"), P(), P()),
        out_specs=P("row", "col"),
        check_vma=False,
    )
```

```python
import functools

import jax
import jax.numpy as jnp
from jax import lax
from jax.experimental import pallas as pl
from jax.experimental.pallas import tpu as pltpu
from jax.sharding import PartitionSpec as P

GROUP = 512
BF16 = jnp.bfloat16
F32 = jnp.float32


VMEM = 127 * 2**19


def after(value, *others):
    return lax.optimization_barrier((value, *others))[0]


def largest_block(size, most):
    return max([b for b in range(16, most + 1, 16) if size % b == 0], default=size)


def send_kernel(ids, turned, core, out):
    out[...] = jnp.dot(turned[...], core[...], preferred_element_type=F32).astype(BF16)


def own_kernel(ids, turned, core, *refs):
    others, (own, out) = refs[:-2], refs[-2:]
    i = pl.program_id(0)
    value = jnp.dot(turned[...], core[...], preferred_element_type=F32)
    for other in others:
        value = value + other[...].astype(F32)

    @pl.when(i == ids[0])
    def _():
        own[...] = value
        out[...] = jnp.zeros_like(out)

    @pl.when(i != ids[0])
    def _():
        out[...] = value.astype(BF16)


def send_block(cols):
    return max(b for b in range(128, 513, 128) if cols % b == 0)


def stage(kernel, ids, turned, core, mask, others, col_size, twins, out_specs, out_shape):
    slots, rows = turned.shape
    cols = core.shape[1] // twins
    block = cols // col_size if others else send_block(cols)
    steps = cols // block
    return pl.pallas_call(
        kernel,
        grid_spec=pltpu.PrefetchScalarGridSpec(
            num_scalar_prefetch=1,
            grid=(steps,),
            in_specs=[
                pl.BlockSpec((slots, rows), lambda j, ids: (0, 0)),
                pl.BlockSpec(
                    (rows, block), lambda j, ids: (0, (ids[1] ^ mask) * steps + j)
                ),
            ]
            + [pl.BlockSpec((slots, block), lambda j, ids: (0, j))] * len(others),
            out_specs=out_specs,
        ),
        out_shape=out_shape,
        cost_estimate=pl.CostEstimate(
            flops=2 * rows * slots * cols,
            bytes_accessed=2 * rows * (cols + slots),
            transcendentals=0,
        ),
        compiler_params=pltpu.CompilerParams(vmem_limit_bytes=VMEM),
        name="own" if others else "send",
    )(ids, turned, core, *others)


def send(ids, turned, core, col_size, twins, flip):
    slots = turned.shape[0]
    part = core.shape[1] // twins // col_size
    result = []
    for mask in range(1, twins):
        if part % 128:
            value = jnp.dot(turned, core, preferred_element_type=F32)
            value = value.reshape(slots, twins, col_size * part)
            value = lax.dynamic_index_in_dim(value, ids[1] ^ mask, 1, keepdims=False)
            value = value.astype(BF16)
        else:
            value = stage(
                send_kernel,
                ids,
                turned,
                core,
                mask,
                [],
                col_size,
                twins,
                pl.BlockSpec((slots, send_block(part * col_size)), lambda j, ids: (0, j)),
                jax.ShapeDtypeStruct((slots, part * col_size), BF16),
            )
        result.append((value, flip(value, mask)))
    return result


def project(ids, turned, core, others, col_size, twins):
    others = [x[1] if isinstance(x, tuple) else x for x in others]
    slots = turned.shape[0]
    part = core.shape[1] // twins // col_size
    k, t = ids[0], ids[1]
    if part % 128:
        value = jnp.dot(turned, core, preferred_element_type=F32)
        value = value.reshape(slots, twins, col_size * part)
        total = lax.dynamic_index_in_dim(value, t, 1, keepdims=False)
        for other in others:
            total = total + other.astype(F32)
        total = jnp.moveaxis(total.reshape(slots, col_size, part), 1, 0)
        own = lax.dynamic_index_in_dim(total, k, 0, keepdims=False)
        mine = jnp.arange(col_size)[:, None, None] == k
        return own, jnp.where(mine, 0, total).astype(BF16)
    return stage(
        own_kernel,
        ids,
        turned,
        core,
        0,
        others,
        col_size,
        twins,
        [
            pl.BlockSpec((slots, part), lambda j, ids: (0, 0)),
            pl.BlockSpec((None, slots, part), lambda j, ids: (j, 0, 0)),
        ],
        [
            jax.ShapeDtypeStruct((slots, part), F32),
            jax.ShapeDtypeStruct((col_size, slots, part), BF16),
        ],
    )


def finish_kernel(own, others, out):
    value = own[...]
    for i in range(others.shape[0]):
        value = value + others[i].astype(F32)
    out[...] = value.astype(BF16)


def finish(own, others):
    return pl.pallas_call(
        finish_kernel,
        out_shape=jax.ShapeDtypeStruct(own.shape, BF16),
        cost_estimate=pl.CostEstimate(
            flops=others.size,
            bytes_accessed=6 * own.size + 2 * others.size,
            transcendentals=0,
        ),
        compiler_params=pltpu.CompilerParams(vmem_limit_bytes=VMEM),
        name="finish",
    )(own, others)


def update_kernel(masks, twins, spans, places, ids, live, *refs):
    halves = refs[:masks], refs[masks : 2 * masks]
    residual, core, *sources = refs[2 * masks : -4]
    out, scaled, panel, sems = refs[-4:]
    depth, part = halves[0][0].shape
    block = out.shape[0]

    @pl.when(pl.program_id(0) == 0)
    def _():
        copies = []
        for n, (first, twin) in enumerate(places):
            source = sources[n]
            count, height, cols = source.shape
            for r in range(count):
                if twin is None:
                    place = r % twins * (count // twins) + r // twins if count > 1 else 0
                    lane = place * cols
                else:
                    place = (ids[1] ^ twin) * count + (ids[0] ^ r)
                    lane = pl.multiple_of(place * cols, cols)
                copies.append(
                    pltpu.make_async_copy(
                        source.at[r],
                        panel.at[pl.ds(first, height), pl.ds(lane, cols)],
                        sems.at[len(copies)],
                    )
                )
        for copy in copies:
            copy.start()
        slot = lax.broadcasted_iota(jnp.int32, residual.shape, 1)
        limit = jnp.where(slot < GROUP, live[0], live[1])
        inside = jnp.where(slot < GROUP, slot, slot - GROUP)
        weight = (inside < limit).astype(F32) / residual[...]
        weight = jnp.concatenate([weight[:, a:b] for a, b in spans], axis=1)
        for g, pieces in enumerate(halves):
            lanes = slice(g * depth, (g + 1) * depth)
            for p, piece in enumerate(pieces):
                value = piece[...].T.astype(F32) * weight[:, lanes]
                scaled[p * part : (p + 1) * part, lanes] = value.astype(BF16)
        for copy in copies:
            copy.wait()

    rows = pl.ds(pl.multiple_of(pl.program_id(0) * block, block), block)
    out[...] = core[...].astype(F32) + jnp.dot(
        scaled[rows, :], panel[...], preferred_element_type=F32
    )


def update(core, stacked, pieces, spans, residual, panels, places, ids, live, twins):
    masks = len(pieces)
    depth, part = pieces[0].shape
    rows, cols = core.shape
    slots = residual.shape[1]
    block = largest_block(part, 320)
    steps = part // block

    def stacked_index(mask):
        return lambda i, ids, live: (ids[0] ^ ids[2] ^ mask, 0, 0)

    tile = pl.BlockSpec(
        (block, cols),
        lambda i, ids, live: ((ids[0] ^ ids[2] ^ (i // steps)) * steps + i % steps, 0),
    )
    once = pl.Buffered(1)
    in_specs = [
        pl.BlockSpec((None, depth, part), stacked_index(mask), pipeline_mode=once)
        for mask in range(masks)
    ]
    in_specs += [
        pl.BlockSpec(x.shape, lambda i, *_: (0, 0), pipeline_mode=once) for x in pieces
    ]
    in_specs += [pl.BlockSpec(residual.shape, lambda i, *_: (0, 0)), tile]
    in_specs += [pl.BlockSpec(memory_space=pl.ANY)] * len(panels)
    return pl.pallas_call(
        functools.partial(update_kernel, masks, twins, spans, places),
        grid_spec=pltpu.PrefetchScalarGridSpec(
            num_scalar_prefetch=2,
            grid=(masks * steps,),
            in_specs=in_specs,
            out_specs=tile,
            scratch_shapes=[
                pltpu.VMEM((masks * part, slots), BF16),
                pltpu.VMEM((slots, cols), BF16),
                pltpu.SemaphoreType.DMA((sum(x.shape[0] for x in panels),)),
            ],
        ),
        out_shape=jax.ShapeDtypeStruct((rows, cols), F32),
        cost_estimate=pl.CostEstimate(
            flops=2 * rows * cols * slots,
            bytes_accessed=rows * cols * 6 + 2 * cols * slots,
            transcendentals=0,
        ),
        compiler_params=pltpu.CompilerParams(vmem_limit_bytes=VMEM),
        name="update",
    )(ids, live, *[stacked] * masks, *pieces, residual, core, *panels)


def shards(row_size, col_size, core_inverse, core_noncore, residual, group_live):
    rows, cols = core_inverse.shape
    width = core_noncore.shape[1]
    twins = row_size // col_size
    part = rows // col_size
    row, z = lax.axis_index("row"), lax.axis_index("col")
    k, t = row // twins, row % twins
    ids = jnp.stack([k, t, z]).astype(jnp.int32)

    def flip(value, mask):
        return lax.ppermute(value, "row", [(r, r ^ mask) for r in range(row_size)])

    def cross(value, mask):
        pairs = []
        for r in range(row_size):
            for c in range(col_size):
                to_row = c * twins + r % twins
                to_col = (r // twins) ^ c ^ mask
                pairs.append((r * col_size + c, to_row * col_size + to_col))
        return lax.ppermute(value, ("row", "col"), pairs)

    def exchange(value):
        plane = [
            [c * twins + twin for c in range(col_size)] for twin in range(twins)
        ]
        return lax.all_to_all(value, "row", 0, 0, axis_index_groups=plane)

    half = width // 2
    turned = core_noncore.T
    animals = [
        lax.all_gather(turned[i * half : (i + 1) * half], "col", axis=0, tiled=True)
        for i in range(2)
    ]

    def gather_plane(group):
        panel = lax.all_gather(group, "row", axis=0)
        if part % 128:
            panel = panel.reshape(col_size, twins, *group.shape)
            panel = jnp.transpose(panel, (2, 1, 0, 3)).reshape(1, -1, cols)
        return panel

    sent = send(ids, animals[0], core_inverse, col_size, twins, flip)
    own, others = project(ids, animals[0], core_inverse, sent, col_size, twins)
    others = exchange(others)
    sent = send(ids, animals[1], core_inverse, col_size, twins, flip)
    first = finish(after(own, *[x[0] for x in sent]), others)
    levels = lax.all_gather(first, "col", axis=0)
    own, others = project(ids, animals[1], core_inverse, sent, col_size, twins)
    flipped, panels = [], []
    if part % 128 == 0:
        masks = [1 << bit for bit in range(col_size.bit_length() - 1)]
        near = {mask: flip(first, mask * twins) for mask in masks}
        others = after(others, *near.values())
        for mask in range(1, col_size):
            if mask in near:
                flipped.append(near[mask])
            elif mask.bit_count() == 2:
                one = mask & -mask
                cut = first.shape[0] // 2
                flipped.append(
                    jnp.concatenate(
                        [
                            flip(near[one][:cut], (mask ^ one) * twins),
                            flip(near[mask ^ one][cut:], one * twins),
                        ]
                    )
                )
            else:
                flipped.append(flip(first, mask * twins))
        held = jnp.stack([first, *flipped])
        panels = [held] + [flip(held, twin) for twin in range(1, twins)]
    second = finish(own, exchange(others))
    crossed = [cross(second, mask) for mask in range(col_size)]
    stacked = exchange(levels)
    if flipped:
        places = [(0, twin) for twin in range(twins)]
        panels.append(gather_plane(second))
        places.append((first.shape[0], None))
    else:
        panels = [gather_plane(jnp.concatenate([first, second], axis=0))]
        places = [(0, None)]

    starts = [q * width + g * half for g in range(2) for q in range(col_size)]
    return update(
        core_inverse,
        stacked,
        crossed,
        [(a, a + half) for a in starts],
        residual[None, :],
        panels,
        places,
        ids,
        group_live,
        twins,
    )


def solution(mesh):
    return jax.shard_map(
        functools.partial(shards, mesh.shape["row"], mesh.shape["col"]),
        mesh=mesh,
        in_specs=(P("row", "col"), P("row", "col"), P(), P()),
        out_specs=P("row", "col"),
        check_vma=False,
    )
```
